32 devices in a mesh: groups: 2 (over y), expert: 16 (over z, x, core), tensor: 1.
Axes of the slice: x: 2, y: 2, z: 4, core: 2. Of those that a mesh axis runs over, the one named last changes fastest.
Arguments:
- tokens: bfloat16 [256, 2048], P(('groups', 'expert', 'tensor')), parts along dimension 0, may hold values from -6 to 6
- routes: int32 [256, 8], P(('groups', 'expert')), parts along dimension 0, may hold values from 0 to 15, all different within a row; in each aligned block of 8 rows (0 to 7, 8 to 15, ...) at most 8 rows name the same one
- combine: float32 [256, 8], P(('groups', 'expert')), parts along dimension 0, may hold values from 0.1 to 1
- prune_mask: int32 [16, 6], P('expert', 'tensor'), may hold values 0 or 1
- gate_weight: bfloat16 [16, 2048, 768], P('expert', None, 'tensor'), may hold values from -0.125 to 0.125
- up_weight: bfloat16 [16, 2048, 768], P('expert', None, 'tensor'), may hold values from -0.125 to 0.125
- down_weight: bfloat16 [16, 768, 2048], P('expert', 'tensor'), may hold values from -0.21875 to 0.21875
Outputs:
- mixed: bfloat16 [256, 2048], P(('groups', 'expert', 'tensor')), parts along dimension 0
The draws below stay inside these ranges and needn't reach their ends.
There are 2 independent parts, one for each index of `groups`. The reference program is written for one: setup_inputs(seed, part) draws one part's arguments, and reference() takes and returns one part's arrays. A program takes and returns all parts, laid end to end along the dimension named above; an argument that names none is the same for every part. Nothing has to cross between parts.
Inputs may be any that keep to these rules, and one draw needn't show every extreme that they name: `routes`: each row names 8 different experts; in each aligned block of 8 rows no expert is named by more than 8 rows. `prune_mask`: 1 keeps a block of 128 hidden units, 0 prunes it.
All inputs are finite; a program needn't handle non-finite values.
Results may differ from the reference program's by a relative error of at most 0.011.
Values may be sent and summed in bfloat16 or wider, within the bound.
No kernel may reach another device: no remote copies, remote signals or barrier semaphores. Data moves between devices by JAX's collectives and lax.ppermute only.
A program may use at most 192 MiB of HBM per device.

```python
import math
import jax
import jax.numpy as jnp
import numpy as np
from jax import lax

D = 2048
FF = 768
TOP = 8
BLK = 128
TOK_DEV = 8
EXPERTS = 16
TOKENS = 128
CAP = 8
NB = 6
N_EXPERT = 16
N_TENSOR = 1


def set_ends(result, key, least, largest):
    longest = result.shape.index(max(result.shape))
    spots = []
    for shift in (0, 1):
        where = [jax.random.randint(jax.random.fold_in(key, axis), (), 0, length) for axis, length in enumerate(result.shape)]
        where[longest] = (where[longest] + shift) % result.shape[longest]
        spots.append(tuple(where))
    return result.at[spots[0]].set(least).at[spots[1]].set(largest)


def shard_levels(rng, extent, cuts, least, top_value):
    level, own = 1.0, jax.random.fold_in(rng, 6)
    for position, parts in cuts:
        steps = jnp.exp(jax.random.uniform(jax.random.fold_in(own, position), (parts,), jnp.float32, least / len(cuts), top_value / len(cuts)))
        level = level * jnp.repeat(steps, extent[position] // parts).reshape([-1 if axis == position else 1 for axis in range(len(extent))])
    return level


def routed_block(key, own, number, rows, number_of, top, limit, slope):
    order = jax.random.permutation(key, number_of)
    crowded, ordinary = load_shares(number_of, rows * top, limit, slope, True), load_shares(number_of, rows * top, limit, slope, False)
    places = jnp.arange(number_of)

    def named(sizes, turn):
        used = int((sizes > 0).sum())
        fixed = max(1, used // 4)
        moved = fixed + (places - fixed + turn * (used - fixed)) % max(1, number_of - fixed)
        return jnp.zeros((number_of,), jnp.int32).at[order[jnp.where(places < fixed, places, moved)]].set(jnp.asarray(sizes, jnp.int32))

    sizes = jnp.where(number % 4 == 0, named(crowded, number // 4), named(ordinary, number - number // 4 - 1))
    mixed = jax.random.permutation(jax.random.fold_in(own, 3), number_of)
    donor, taker = mixed[0:number_of // 2 * 2:2], mixed[1:number_of // 2 * 2:2]
    slack = jnp.minimum(sizes[donor] - 1, limit - sizes[taker]) // 2
    slack = jnp.where((donor == order[0]) | (taker == order[0]) | (sizes[taker] == 0), 0, jnp.maximum(slack, 0))
    moved = jax.random.randint(jax.random.fold_in(own, 4), (number_of // 2,), 0, 1 << 20) % (slack + 1)
    sizes = sizes.at[donor].add(-moved).at[taker].add(moved)
    members = jnp.searchsorted(jnp.cumsum(sizes), jnp.arange(rows * top), side="right").astype(jnp.int32)
    listing = members.reshape(top, rows).T
    listing = listing[jax.random.permutation(jax.random.fold_in(own, 1), rows)]
    turn = jax.random.randint(jax.random.fold_in(own, 2), (rows, 1), 0, top)
    return jnp.take_along_axis(listing, (jnp.arange(top)[None, :] + turn) % top, axis=1)


def load_shares(count, total, most, slope, full):
    weights = [(1 << 20) // math.isqrt(rank ** slope) + 1 for rank in range(1, count + 1)]
    largest = most if full else min(most, max(-(-total // count), total * weights[0] // sum(weights)))
    least = 1 if total - largest >= count - 1 else 0
    holding, rest = [largest] + [least] * (count - 1), total - largest - least * (count - 1)
    while rest > 0:
        free = [i for i in range(1, count) if holding[i] < largest] or [i for i in range(1, count) if holding[i] < most]
        mass, budget = sum([weights[i] for i in free]), rest
        for i in free:
            more = min(most - holding[i], max(1, budget * weights[i] // mass), rest)
            holding[i] = holding[i] + more
            rest = rest - more
    return np.array(holding)


def scatter_about(rng, shape, scale, limit, pieces=(), held_as=jnp.bfloat16):
    factor_of = shard_levels(rng, shape, pieces, -0.22, 0.18) if pieces else 1.0
    values = jax.random.normal(rng, shape, jnp.float32) * scale * factor_of
    return jnp.minimum(jnp.maximum(values, -limit), limit).astype(held_as)


def setup_inputs(seed: int = 0, part: int = 0) -> dict:
    streams_of = jax.random.split(jax.random.key(seed), 8)
    own_keys = jax.random.split(jax.random.fold_in(streams_of[7], part), 8)
    tokens = scatter_about(own_keys[0], (TOKENS, D), 1.0, 6.0, ((0, 16),))
    routes_keys = jax.random.split(jax.random.fold_in(own_keys[1], 1), TOKENS // (N_TENSOR * TOK_DEV))
    routes_turns = jax.random.permutation(jax.random.fold_in(own_keys[1], 3), TOKENS // (N_TENSOR * TOK_DEV))
    routes = jax.vmap(lambda own, number: routed_block(jax.random.fold_in(own_keys[1], 2), own, number, N_TENSOR * TOK_DEV, EXPERTS, TOP, CAP, 2))(routes_keys, routes_turns).reshape((TOKENS, TOP))
    combine = jnp.clip(jnp.exp(math.log(1.0) - 2.3025851 * jax.random.uniform(own_keys[2], (TOKENS, TOP), jnp.float32) ** shard_levels(own_keys[2], (TOKENS, TOP), ((0, 16),), -0.2, 0.2)), 0.1, 1.0)
    prune_mask = set_ends((jax.random.randint(streams_of[3], (EXPERTS, NB), 0, 4) < 3).astype(jnp.int32), jax.random.fold_in(streams_of[3], 1), 0, 1)
    gate_weight = scatter_about(streams_of[4], (EXPERTS, D, FF), D ** -0.5, 0.125, ((0, 16),))
    up_weight = scatter_about(streams_of[5], (EXPERTS, D, FF), D ** -0.5, 0.125, ((0, 16),))
    down_weight = scatter_about(streams_of[6], (EXPERTS, FF, D), FF ** -0.5, 0.21875, ((0, 16),))
    return dict(tokens=tokens, routes=routes, combine=combine, prune_mask=prune_mask, gate_weight=gate_weight, up_weight=up_weight, down_weight=down_weight)


def reference(tokens, routes, combine, prune_mask, gate_weight, up_weight, down_weight):
    flat_routes = routes.reshape(-1)
    flat_weights = combine.reshape(-1)
    slot_count = N_EXPERT * CAP
    half_units = FF // N_TENSOR

    def per_expert(summed, expert_items):
        expert, gate_e, up_e, down_e, keep_e = expert_items
        chosen = flat_routes == expert
        places = jnp.nonzero(chosen, size=slot_count, fill_value=0)[0].astype(jnp.int32)
        row_count = jnp.sum(chosen.astype(jnp.int32))
        live_slots = jnp.arange(slot_count, dtype=jnp.int32) < row_count
        owners = places // TOP
        row_feats = tokens[owners]
        gate_act = jnp.dot(row_feats, gate_e, preferred_element_type=jnp.float32)
        up_act = jnp.dot(row_feats, up_e, preferred_element_type=jnp.float32)
        keep_cols = jnp.repeat(keep_e.astype(jnp.float32), BLK)
        hidden = (jax.nn.silu(gate_act) * up_act * keep_cols).astype(jnp.bfloat16)
        added = jnp.zeros((slot_count, tokens.shape[1]), jnp.float32)
        for half_index in range(N_TENSOR):
            lower = half_index * half_units
            part_out = jnp.dot(hidden[:, lower:lower + half_units], down_e[lower:lower + half_units], preferred_element_type=jnp.float32)
            rounded = lax.optimization_barrier(part_out.astype(jnp.bfloat16))
            added = added + rounded.astype(jnp.float32)
        expert_out = added.astype(jnp.bfloat16)
        weights = jnp.where(live_slots, flat_weights[places], jnp.float32(0.0))
        summed = summed.at[owners].add(expert_out.astype(jnp.float32) * weights[:, None])
        return summed, None

    expert_ids = jnp.arange(EXPERTS, dtype=jnp.int32)
    start = jnp.zeros(tokens.shape, jnp.float32)
    summed, _ = lax.scan(per_expert, start, (expert_ids, gate_weight, up_weight, down_weight, prune_mask))
    return summed.astype(jnp.bfloat16)
```

```python
import jax
import jax.numpy as jnp
from jax import lax
from jax.sharding import PartitionSpec as P

BLK = 128


def slot_places(group_routes, experts, capacity):
    flat_routes = group_routes.reshape(-1)
    onehot = (flat_routes[:, None] == jnp.arange(experts, dtype=jnp.int32)[None, :]).astype(
        jnp.int32
    )
    before = jnp.cumsum(onehot, axis=0) - onehot
    slot_index = jnp.sum(before * onehot, axis=1)
    return flat_routes * capacity + slot_index


def fill_slots(row_source, places, experts, capacity, top_k):
    owners = jnp.full((experts * capacity,), -1, jnp.int32)
    owners = owners.at[places].set(jnp.arange(places.shape[0], dtype=jnp.int32) // top_k)
    filled = owners >= 0
    outgoing = row_source[jnp.maximum(owners, 0)]
    outgoing = jnp.where(filled[:, None], outgoing, jnp.zeros_like(outgoing))
    return outgoing.reshape(experts, capacity, row_source.shape[1])


def expert_partial(row_block, gate_weight, up_weight, down_weight, prune_mask):
    keep_cols = jnp.repeat(prune_mask[0].astype(jnp.float32), BLK)
    gate_act = jnp.dot(row_block, gate_weight[0], preferred_element_type=jnp.float32)
    up_act = jnp.dot(row_block, up_weight[0], preferred_element_type=jnp.float32)
    hidden = (jax.nn.silu(gate_act) * up_act * keep_cols).astype(jnp.bfloat16)
    partial_value = jnp.dot(hidden, down_weight[0], preferred_element_type=jnp.float32)
    rounded = lax.optimization_barrier(partial_value.astype(jnp.bfloat16))
    return rounded.astype(jnp.float32)


def slotted_body(tokens, routes, combine, prune_mask, gate_weight, up_weight, down_weight):
    tok_dev, model_width = tokens.shape
    group_rows, top_k = routes.shape
    experts = lax.axis_size("expert")
    capacity = min(group_rows, 2 * group_rows * top_k // experts)
    places = slot_places(routes, experts, capacity)
    pair_rows = lax.all_gather(tokens, "tensor", axis=0, tiled=True)
    outgoing = fill_slots(pair_rows, places, experts, capacity, top_k)
    received = lax.all_to_all(outgoing, "expert", split_axis=0, concat_axis=0, tiled=True)
    item_count = received.shape[1]
    partial_value = expert_partial(
        received.reshape(-1, model_width), gate_weight, up_weight, down_weight, prune_mask
    )
    whole_sum = lax.psum(partial_value.astype(jnp.bfloat16), "tensor")
    answers = whole_sum.reshape(experts, item_count, model_width)
    returned = lax.all_to_all(answers, "expert", split_axis=0, concat_axis=0, tiled=True).reshape(
        -1, model_width
    )
    member = lax.axis_index("tensor")
    own_places = lax.dynamic_slice_in_dim(places, member * tok_dev * top_k, tok_dev * top_k, 0)
    own_weights = lax.dynamic_slice_in_dim(combine, member * tok_dev, tok_dev, 0)
    picked = returned[own_places].reshape(tok_dev, top_k, model_width).astype(jnp.float32)
    mixed_out = jnp.einsum("tk,tkd->td", own_weights, picked)
    return mixed_out.astype(jnp.bfloat16)


def exact_parts(values):
    high = values.astype(jnp.bfloat16)
    rest = values - high.astype(jnp.float32)
    middle = rest.astype(jnp.bfloat16)
    low = (rest - middle.astype(jnp.float32)).astype(jnp.bfloat16)
    return high, middle, low


def swap(block, distance, experts):
    return lax.ppermute(block, "expert", [(i, i ^ distance) for i in range(experts)])


def dense_body(tokens, routes, combine, prune_mask, gate_weight, up_weight, down_weight):
    tok_dev, model_width = tokens.shape
    experts = lax.axis_size("expert")
    me = lax.axis_index("expert")
    chosen = routes[:, :, None] == jnp.arange(experts, dtype=jnp.int32)[None, None, :]
    shares = jnp.sum(jnp.where(chosen, combine[:, :, None], 0.0), axis=1)
    extra = jnp.concatenate(exact_parts(shares), axis=1)
    extra = jnp.pad(extra, ((0, 0), (0, -extra.shape[1] % 128)))
    rows = jnp.concatenate([tokens, extra], axis=1)
    distances = [1 << bit for bit in range(experts.bit_length() - 1)]
    for distance in reversed(distances):
        rows = jnp.concatenate([rows, swap(rows, distance, experts)], axis=0)
    lane = jnp.arange(extra.shape[1], dtype=jnp.int32)[None, :]
    mine = (lane % experts == me) & (lane < 3 * experts)
    share = jnp.sum(jnp.where(mine, rows[:, model_width:].astype(jnp.float32), 0.0), axis=1)
    keep_cols = jnp.repeat(prune_mask[0].astype(jnp.float32), BLK)
    row_block = rows[:, :model_width]
    gate_act = jnp.dot(row_block, gate_weight[0], preferred_element_type=jnp.float32)
    up_act = jnp.dot(row_block, up_weight[0], preferred_element_type=jnp.float32)
    hidden = (jax.nn.silu(gate_act) * up_act * keep_cols).astype(jnp.bfloat16)
    answers = jnp.dot(hidden, down_weight[0], preferred_element_type=jnp.float32)
    sums = (answers * share[:, None]).astype(jnp.bfloat16)
    for distance in distances:
        half = sums.shape[0] // 2
        arrived = swap(sums[half:], distance, experts)
        sums = (sums[:half].astype(jnp.float32) + arrived.astype(jnp.float32)).astype(jnp.bfloat16)
    return sums


def body(tokens, routes, combine, prune_mask, gate_weight, up_weight, down_weight):
    experts = lax.axis_size("expert")
    group_rows, top_k = routes.shape
    full = 2 * group_rows * top_k // experts >= group_rows
    paired = experts & (experts - 1) == 0
    if full and paired and lax.axis_size("tensor") == 1:
        chosen_body = dense_body
    else:
        chosen_body = slotted_body
    return chosen_body(tokens, routes, combine, prune_mask, gate_weight, up_weight, down_weight)


def solution(mesh):
    in_specs = (
        P(("groups", "expert", "tensor"), None),
        P(("groups", "expert"), None),
        P(("groups", "expert"), None),
        P("expert", "tensor"),
        P("expert", None, "tensor"),
        P("expert", None, "tensor"),
        P("expert", "tensor", None),
    )
    out_specs = P(("groups", "expert", "tensor"), None)
    return jax.shard_map(body, mesh=mesh, in_specs=in_specs, out_specs=out_specs, check_vma=False)
```

```python
import functools

import jax
import jax.numpy as jnp
from jax import lax
from jax.experimental import pallas as pl
from jax.experimental.pallas import tpu as pltpu
from jax.sharding import PartitionSpec as P

BLK = 128


def slot_places(group_routes, experts, capacity):
    flat_routes = group_routes.reshape(-1)
    onehot = (flat_routes[:, None] == jnp.arange(experts, dtype=jnp.int32)[None, :]).astype(
        jnp.int32
    )
    before = jnp.cumsum(onehot, axis=0) - onehot
    slot_index = jnp.sum(before * onehot, axis=1)
    return flat_routes * capacity + slot_index


def fill_slots(row_source, places, experts, capacity, top_k):
    owners = jnp.full((experts * capacity,), -1, jnp.int32)
    owners = owners.at[places].set(jnp.arange(places.shape[0], dtype=jnp.int32) // top_k)
    filled = owners >= 0
    outgoing = row_source[jnp.maximum(owners, 0)]
    outgoing = jnp.where(filled[:, None], outgoing, jnp.zeros_like(outgoing))
    return outgoing.reshape(experts, capacity, row_source.shape[1])


def expert_partial(row_block, gate_weight, up_weight, down_weight, prune_mask):
    keep_cols = jnp.repeat(prune_mask[0].astype(jnp.float32), BLK)
    gate_act = jnp.dot(row_block, gate_weight[0], preferred_element_type=jnp.float32)
    up_act = jnp.dot(row_block, up_weight[0], preferred_element_type=jnp.float32)
    hidden = (jax.nn.silu(gate_act) * up_act * keep_cols).astype(jnp.bfloat16)
    partial_value = jnp.dot(hidden, down_weight[0], preferred_element_type=jnp.float32)
    rounded = lax.optimization_barrier(partial_value.astype(jnp.bfloat16))
    return rounded.astype(jnp.float32)


def slotted_body(tokens, routes, combine, prune_mask, gate_weight, up_weight, down_weight):
    tok_dev, model_width = tokens.shape
    group_rows, top_k = routes.shape
    experts = lax.axis_size("expert")
    capacity = min(group_rows, 2 * group_rows * top_k // experts)
    places = slot_places(routes, experts, capacity)
    pair_rows = lax.all_gather(tokens, "tensor", axis=0, tiled=True)
    outgoing = fill_slots(pair_rows, places, experts, capacity, top_k)
    received = lax.all_to_all(outgoing, "expert", split_axis=0, concat_axis=0, tiled=True)
    item_count = received.shape[1]
    partial_value = expert_partial(
        received.reshape(-1, model_width), gate_weight, up_weight, down_weight, prune_mask
    )
    whole_sum = lax.psum(partial_value.astype(jnp.bfloat16), "tensor")
    answers = whole_sum.reshape(experts, item_count, model_width)
    returned = lax.all_to_all(answers, "expert", split_axis=0, concat_axis=0, tiled=True).reshape(
        -1, model_width
    )
    member = lax.axis_index("tensor")
    own_places = lax.dynamic_slice_in_dim(places, member * tok_dev * top_k, tok_dev * top_k, 0)
    own_weights = lax.dynamic_slice_in_dim(combine, member * tok_dev, tok_dev, 0)
    picked = returned[own_places].reshape(tok_dev, top_k, model_width).astype(jnp.float32)
    mixed_out = jnp.einsum("tk,tkd->td", own_weights, picked)
    return mixed_out.astype(jnp.bfloat16)


WHOLE = pl.BlockSpec(memory_space=pltpu.VMEM)
ANYWHERE = pl.BlockSpec(memory_space=pl.ANY)


def swap(block, distance, experts):
    return lax.ppermute(block, "expert", [(i, i ^ distance) for i in range(experts)])


def joined(*blocks):
    return lax.optimization_barrier(jnp.concatenate(blocks, axis=0))


def add(a, b):
    return (a.astype(jnp.float32) + b.astype(jnp.float32)).astype(jnp.bfloat16)


def pack_kernel(tokens_ref, share_ref, out_ref):
    width = tokens_ref.shape[1]
    share = share_ref[...]
    experts = share.shape[1] // 3
    high = share.astype(jnp.bfloat16).astype(jnp.float32)
    middle = (share - high).astype(jnp.bfloat16).astype(jnp.float32)
    low = share - high - middle
    part = lax.broadcasted_iota(jnp.int32, share.shape, 1) // experts
    extra = jnp.where(part == 0, high, jnp.where(part == 1, middle, low))
    out_ref[:, :width] = tokens_ref[...]
    out_ref[:, width:] = jnp.zeros((tokens_ref.shape[0], out_ref.shape[1] - width), jnp.bfloat16)
    out_ref[:, width : width + 3 * experts] = extra.astype(jnp.bfloat16)


def load_kernel(source, after, target, sems):
    del after
    count = sems.shape[0]
    rows = source.shape[1] // count
    copies = [
        pltpu.make_async_copy(source.at[:, i * rows : (i + 1) * rows], target.at[:, i * rows : (i + 1) * rows], sems.at[i])
        for i in range(count)
    ]
    for copy in copies:
        copy.start()
    for copy in copies:
        copy.wait()


def load(source, after):
    return pl.pallas_call(
        load_kernel,
        out_shape=jax.ShapeDtypeStruct(source.shape, source.dtype),
        in_specs=[ANYWHERE] * 2,
        out_specs=WHOLE,
        scratch_shapes=[pltpu.SemaphoreType.DMA((4,))],
        cost_estimate=pl.CostEstimate(flops=0, bytes_accessed=2 * source.size, transcendentals=0),
        compiler_params=pltpu.CompilerParams(vmem_limit_bytes=1 << 20),
    )(source, after)


def expert_kernel(experts, n_pieces, *refs):
    pieces = refs[:n_pieces]
    mask_ref, gate_ref, up_ref, down_ref, keep_ref, send_ref, rows, hidden = refs[n_pieces:]
    width, units = gate_ref.shape[1:]
    me = lax.axis_index("expert")
    spots = []
    at = 0
    for piece in pieces:
        count = piece.shape[0]
        rows[at : at + count, :] = piece[:, :width]
        extra = piece[:, width:]
        lane = lax.broadcasted_iota(jnp.int32, extra.shape, 1)
        mine = (lane % experts == me) & (lane < 3 * experts)
        spots.append(jnp.sum(jnp.where(mine, extra.astype(jnp.float32), 0.0), axis=1, keepdims=True))
        at += count
    share = jnp.concatenate(spots, axis=0)
    for j in range(units // BLK):
        cols = slice(j * BLK, (j + 1) * BLK)
        keep = mask_ref[0, j].astype(jnp.float32)
        gate_act = jnp.dot(rows[...], gate_ref[0, :, cols], preferred_element_type=jnp.float32)
        up_act = jnp.dot(rows[...], up_ref[0, :, cols], preferred_element_type=jnp.float32)
        value = gate_act / (1.0 + jnp.exp(-gate_act)) * up_act * keep
        hidden[:, cols] = value.astype(jnp.bfloat16)
    half = rows.shape[0] // 2
    step = 512 if width % 512 == 0 else BLK
    for j in range(width // step):
        cols = slice(j * step, (j + 1) * step)
        answer = jnp.dot(hidden[...], down_ref[0, :, cols], preferred_element_type=jnp.float32)
        answer = (answer * share).astype(jnp.bfloat16)
        keep_ref[:, cols] = answer[:half]
        send_ref[:, cols] = answer[half:]


def dense_body(tokens, routes, combine, prune_mask, gate_weight, up_weight, down_weight):
    tok_dev, model_width = tokens.shape
    units = gate_weight.shape[2]
    experts = lax.axis_size("expert")
    distances = [1 << bit for bit in range(experts.bit_length() - 1)]
    lanes = jnp.arange(3 * experts, dtype=jnp.int32) % experts
    chosen = routes[:, :, None] == lanes[None, None, :]
    shares = jnp.sum(jnp.where(chosen, combine[:, :, None], 0.0), axis=1)
    rows = pl.pallas_call(
        pack_kernel,
        out_shape=jax.ShapeDtypeStruct((tok_dev, model_width + BLK), jnp.bfloat16),
        in_specs=[WHOLE] * 2,
        out_specs=WHOLE,
        compiler_params=pltpu.CompilerParams(vmem_limit_bytes=1 << 20),
    )(tokens, shares)
    weights = []
    for distance, weight in zip(reversed(distances[1:]), (gate_weight, up_weight, down_weight)):
        loaded = load(weight, rows)
        both = jnp.concatenate([rows, swap(rows, distance, experts)], axis=0)
        rows, loaded = lax.optimization_barrier((both, loaded))
        weights.append(loaded)
    pieces = [rows, swap(rows, distances[0], experts)]
    total = sum(piece.shape[0] for piece in pieces)
    out = jax.ShapeDtypeStruct((total // 2, model_width), jnp.bfloat16)
    kept, sent = pl.pallas_call(
        functools.partial(expert_kernel, experts, len(pieces)),
        out_shape=(out, out),
        in_specs=[WHOLE] * len(pieces) + [pl.BlockSpec(memory_space=pltpu.SMEM)] + [WHOLE] * 3,
        out_specs=(WHOLE, WHOLE),
        scratch_shapes=[pltpu.VMEM((total, model_width), jnp.bfloat16), pltpu.VMEM((total, units), jnp.bfloat16)],
        compiler_params=pltpu.CompilerParams(vmem_limit_bytes=16 << 20),
    )(*pieces, prune_mask, *weights)
    arrived = swap(sent, distances[0], experts)
    for distance in distances[1:]:
        half = kept.shape[0] // 2
        sent = lax.optimization_barrier(add(kept[half:], arrived[half:]))
        kept = add(kept[:half], arrived[:half])
        arrived = swap(sent, distance, experts)
    return add(kept, arrived)


def body(tokens, routes, combine, prune_mask, gate_weight, up_weight, down_weight):
    experts = lax.axis_size("expert")
    group_rows, top_k = routes.shape
    full = 2 * group_rows * top_k // experts >= group_rows
    if full and experts == 16 and lax.axis_size("tensor") == 1:
        chosen_body = dense_body
    else:
        chosen_body = slotted_body
    return chosen_body(tokens, routes, combine, prune_mask, gate_weight, up_weight, down_weight)


def solution(mesh):
    in_specs = (
        P(("groups", "expert", "tensor"), None),
        P(("groups", "expert"), None),
        P(("groups", "expert"), None),
        P("expert", "tensor"),
        P("expert", None, "tensor"),
        P("expert", None, "tensor"),
        P("expert", "tensor", None),
    )
    out_specs = P(("groups", "expert", "tensor"), None)
    return jax.shard_map(body, mesh=mesh, in_specs=in_specs, out_specs=out_specs, check_vma=False)
```

```python
import functools

import jax
import jax.numpy as jnp
from jax import lax
from jax.experimental import pallas as pl
from jax.experimental.pallas import tpu as pltpu
from jax.sharding import PartitionSpec as P

BLK = 128


def slot_places(group_routes, experts, capacity):
    flat_routes = group_routes.reshape(-1)
    onehot = (flat_routes[:, None] == jnp.arange(experts, dtype=jnp.int32)[None, :]).astype(
        jnp.int32
    )
    before = jnp.cumsum(onehot, axis=0) - onehot
    slot_index = jnp.sum(before * onehot, axis=1)
    return flat_routes * capacity + slot_index


def fill_slots(row_source, places, experts, capacity, top_k):
    owners = jnp.full((experts * capacity,), -1, jnp.int32)
    owners = owners.at[places].set(jnp.arange(places.shape[0], dtype=jnp.int32) // top_k)
    filled = owners >= 0
    outgoing = row_source[jnp.maximum(owners, 0)]
    outgoing = jnp.where(filled[:, None], outgoing, jnp.zeros_like(outgoing))
    return outgoing.reshape(experts, capacity, row_source.shape[1])


def expert_partial(row_block, gate_weight, up_weight, down_weight, prune_mask):
    keep_cols = jnp.repeat(prune_mask[0].astype(jnp.float32), BLK)
    gate_act = jnp.dot(row_block, gate_weight[0], preferred_element_type=jnp.float32)
    up_act = jnp.dot(row_block, up_weight[0], preferred_element_type=jnp.float32)
    hidden = (jax.nn.silu(gate_act) * up_act * keep_cols).astype(jnp.bfloat16)
    partial_value = jnp.dot(hidden, down_weight[0], preferred_element_type=jnp.float32)
    rounded = lax.optimization_barrier(partial_value.astype(jnp.bfloat16))
    return rounded.astype(jnp.float32)


def slotted_body(tokens, routes, combine, prune_mask, gate_weight, up_weight, down_weight):
    tok_dev, model_width = tokens.shape
    group_rows, top_k = routes.shape
    experts = lax.axis_size("expert")
    capacity = min(group_rows, 2 * group_rows * top_k // experts)
    places = slot_places(routes, experts, capacity)
    pair_rows = lax.all_gather(tokens, "tensor", axis=0, tiled=True)
    outgoing = fill_slots(pair_rows, places, experts, capacity, top_k)
    received = lax.all_to_all(outgoing, "expert", split_axis=0, concat_axis=0, tiled=True)
    item_count = received.shape[1]
    partial_value = expert_partial(
        received.reshape(-1, model_width), gate_weight, up_weight, down_weight, prune_mask
    )
    whole_sum = lax.psum(partial_value.astype(jnp.bfloat16), "tensor")
    answers = whole_sum.reshape(experts, item_count, model_width)
    returned = lax.all_to_all(answers, "expert", split_axis=0, concat_axis=0, tiled=True).reshape(
        -1, model_width
    )
    member = lax.axis_index("tensor")
    own_places = lax.dynamic_slice_in_dim(places, member * tok_dev * top_k, tok_dev * top_k, 0)
    own_weights = lax.dynamic_slice_in_dim(combine, member * tok_dev, tok_dev, 0)
    picked = returned[own_places].reshape(tok_dev, top_k, model_width).astype(jnp.float32)
    mixed_out = jnp.einsum("tk,tkd->td", own_weights, picked)
    return mixed_out.astype(jnp.bfloat16)


WHOLE = pl.BlockSpec(memory_space=pltpu.VMEM)
ANYWHERE = pl.BlockSpec(memory_space=pl.ANY)


def swap(block, distance, experts):
    return lax.ppermute(block, "expert", [(i, i ^ distance) for i in range(experts)])


def swap_apart(block, even, odd, experts):
    return lax.ppermute(block, "expert", [(i, i ^ (odd if i % 2 else even)) for i in range(experts)])


def joined(a, b, loaded):
    return lax.optimization_barrier((jnp.concatenate([a, b], axis=0), loaded))


def add(*blocks):
    return functools.reduce(jnp.add, [block.astype(jnp.float32) for block in blocks]).astype(jnp.bfloat16)


def pack_kernel(tokens_ref, share_ref, out_ref):
    width = tokens_ref.shape[1]
    share = share_ref[...]
    experts = share.shape[1] // 3
    high = share.astype(jnp.bfloat16).astype(jnp.float32)
    middle = (share - high).astype(jnp.bfloat16).astype(jnp.float32)
    low = share - high - middle
    part = lax.broadcasted_iota(jnp.int32, share.shape, 1) // experts
    extra = jnp.where(part == 0, high, jnp.where(part == 1, middle, low))
    out_ref[:, :width] = tokens_ref[...]
    out_ref[:, width:] = jnp.zeros((tokens_ref.shape[0], out_ref.shape[1] - width), jnp.bfloat16)
    out_ref[:, width : width + 3 * experts] = extra.astype(jnp.bfloat16)


def load_kernel(source, after, target, sems):
    del after
    count = sems.shape[0]
    rows = source.shape[1] // count
    copies = [
        pltpu.make_async_copy(source.at[:, i * rows : (i + 1) * rows], target.at[:, i * rows : (i + 1) * rows], sems.at[i])
        for i in range(count)
    ]
    for copy in copies:
        copy.start()
    for copy in copies:
        copy.wait()


def load(source, after):
    return pl.pallas_call(
        load_kernel,
        out_shape=jax.ShapeDtypeStruct(source.shape, source.dtype),
        in_specs=[ANYWHERE] * 2,
        out_specs=WHOLE,
        scratch_shapes=[pltpu.SemaphoreType.DMA((4,))],
        cost_estimate=pl.CostEstimate(flops=0, bytes_accessed=2 * source.size, transcendentals=0),
        compiler_params=pltpu.CompilerParams(vmem_limit_bytes=1 << 20),
    )(source, after)


def expert_kernel(experts, n_pieces, *refs):
    pieces = refs[:n_pieces]
    mask_ref, gate_ref, up_ref, down_ref = refs[n_pieces : n_pieces + 4]
    answers = refs[n_pieces + 4 : 2 * n_pieces + 4]
    rows, hidden = refs[2 * n_pieces + 4 :]
    width, units = gate_ref.shape[1:]
    me = lax.axis_index("expert")
    spots, spans = [], []
    at = 0
    for piece in pieces:
        count = piece.shape[0]
        spans.append(slice(at, at + count))
        rows[at : at + count, :] = piece[:, :width]
        extra = piece[:, width:]
        lane = lax.broadcasted_iota(jnp.int32, extra.shape, 1)
        mine = (lane % experts == me) & (lane < 3 * experts)
        spots.append(jnp.sum(jnp.where(mine, extra.astype(jnp.float32), 0.0), axis=1, keepdims=True))
        at += count
    share = jnp.concatenate(spots, axis=0)
    for j in range(units // BLK):
        cols = slice(j * BLK, (j + 1) * BLK)
        keep = mask_ref[0, j].astype(jnp.float32)
        gate_act = jnp.dot(rows[...], gate_ref[0, :, cols], preferred_element_type=jnp.float32)
        up_act = jnp.dot(rows[...], up_ref[0, :, cols], preferred_element_type=jnp.float32)
        value = gate_act / (1.0 + jnp.exp(-gate_act)) * up_act * keep
        hidden[:, cols] = value.astype(jnp.bfloat16)
    step = 512 if width % 512 == 0 else BLK
    for j in range(width // step):
        cols = slice(j * step, (j + 1) * step)
        answer = jnp.dot(hidden[...], down_ref[0, :, cols], preferred_element_type=jnp.float32)
        answer = (answer * share).astype(jnp.bfloat16)
        for answer_ref, span in zip(answers, spans):
            answer_ref[:, cols] = answer[span]


def dense_body(tokens, routes, combine, prune_mask, gate_weight, up_weight, down_weight):
    tok_dev, model_width = tokens.shape
    units = gate_weight.shape[2]
    experts = lax.axis_size("expert")
    lanes = jnp.arange(3 * experts, dtype=jnp.int32) % experts
    chosen = routes[:, :, None] == lanes[None, None, :]
    shares = jnp.sum(jnp.where(chosen, combine[:, :, None], 0.0), axis=1)
    packed = pl.pallas_call(
        pack_kernel,
        out_shape=jax.ShapeDtypeStruct((tok_dev, model_width + BLK), jnp.bfloat16),
        in_specs=[WHOLE] * 2,
        out_specs=WHOLE,
        compiler_params=pltpu.CompilerParams(vmem_limit_bytes=1 << 20),
    )(tokens, shares)
    own, gate_here = joined(packed, swap(packed, 8, experts), load(gate_weight, packed))
    across = swap(own, 6, experts)
    chip, up_here = joined(own, swap(own, 1, experts), load(up_weight, own))
    beside = swap_apart(chip, 4, 2, experts)
    beside, down_here = lax.optimization_barrier((beside, load(down_weight, chip)))
    pieces = [chip, beside, across, swap(beside, 1, experts), swap(across, 1, experts)]
    total = sum(piece.shape[0] for piece in pieces)
    chip, beside, across, beside_far, across_far = pl.pallas_call(
        functools.partial(expert_kernel, experts, len(pieces)),
        out_shape=[jax.ShapeDtypeStruct((piece.shape[0], model_width), jnp.bfloat16) for piece in pieces],
        in_specs=[WHOLE] * len(pieces) + [pl.BlockSpec(memory_space=pltpu.SMEM)] + [WHOLE] * 3,
        out_specs=[WHOLE] * len(pieces),
        scratch_shapes=[pltpu.VMEM((total, model_width), jnp.bfloat16), pltpu.VMEM((total, units), jnp.bfloat16)],
        compiler_params=pltpu.CompilerParams(vmem_limit_bytes=16 << 20),
    )(*pieces, prune_mask, gate_here, up_here, down_here)
    half = 2 * tok_dev
    beside = swap_apart(lax.optimization_barrier(add(beside, swap(beside_far, 1, experts))), 4, 2, experts)
    across = swap(lax.optimization_barrier(add(across, swap(across_far, 1, experts))), 6, experts)
    far = swap(lax.optimization_barrier(add(chip[half:], beside[half:])), 1, experts)
    near, beside, across = chip[:half], beside[:half], across
    sent = lax.optimization_barrier(add(near[tok_dev:], beside[tok_dev:], across[tok_dev:], far[tok_dev:]))
    return add(near[:tok_dev], beside[:tok_dev], across[:tok_dev], far[:tok_dev], swap(sent, 8, experts))


def body(tokens, routes, combine, prune_mask, gate_weight, up_weight, down_weight):
    experts = lax.axis_size("expert")
    group_rows, top_k = routes.shape
    full = 2 * group_rows * top_k // experts >= group_rows
    if full and experts == 16 and lax.axis_size("tensor") == 1:
        chosen_body = dense_body
    else:
        chosen_body = slotted_body
    return chosen_body(tokens, routes, combine, prune_mask, gate_weight, up_weight, down_weight)


def solution(mesh):
    in_specs = (
        P(("groups", "expert", "tensor"), None),
        P(("groups", "expert"), None),
        P(("groups", "expert"), None),
        P("expert", "tensor"),
        P("expert", None, "tensor"),
        P("expert", None, "tensor"),
        P("expert", "tensor", None),
    )
    out_specs = P(("groups", "expert", "tensor"), None)
    return jax.shard_map(body, mesh=mesh, in_specs=in_specs, out_specs=out_specs, check_vma=False)
```

```python
import functools

import jax
import jax.numpy as jnp
from jax import lax
from jax.experimental import pallas as pl
from jax.experimental.pallas import tpu as pltpu
from jax.sharding import PartitionSpec as P

BLK = 128


def slot_places(group_routes, experts, capacity):
    flat_routes = group_routes.reshape(-1)
    onehot = (flat_routes[:, None] == jnp.arange(experts, dtype=jnp.int32)[None, :]).astype(
        jnp.int32
    )
    before = jnp.cumsum(onehot, axis=0) - onehot
    slot_index = jnp.sum(before * onehot, axis=1)
    return flat_routes * capacity + slot_index


def fill_slots(row_source, places, experts, capacity, top_k):
    owners = jnp.full((experts * capacity,), -1, jnp.int32)
    owners = owners.at[places].set(jnp.arange(places.shape[0], dtype=jnp.int32) // top_k)
    filled = owners >= 0
    outgoing = row_source[jnp.maximum(owners, 0)]
    outgoing = jnp.where(filled[:, None], outgoing, jnp.zeros_like(outgoing))
    return outgoing.reshape(experts, capacity, row_source.shape[1])


def expert_partial(row_block, gate_weight, up_weight, down_weight, prune_mask):
    keep_cols = jnp.repeat(prune_mask[0].astype(jnp.float32), BLK)
    gate_act = jnp.dot(row_block, gate_weight[0], preferred_element_type=jnp.float32)
    up_act = jnp.dot(row_block, up_weight[0], preferred_element_type=jnp.float32)
    hidden = (jax.nn.silu(gate_act) * up_act * keep_cols).astype(jnp.bfloat16)
    partial_value = jnp.dot(hidden, down_weight[0], preferred_element_type=jnp.float32)
    rounded = lax.optimization_barrier(partial_value.astype(jnp.bfloat16))
    return rounded.astype(jnp.float32)


def slotted_body(tokens, routes, combine, prune_mask, gate_weight, up_weight, down_weight):
    tok_dev, model_width = tokens.shape
    group_rows, top_k = routes.shape
    experts = lax.axis_size("expert")
    capacity = min(group_rows, 2 * group_rows * top_k // experts)
    places = slot_places(routes, experts, capacity)
    pair_rows = lax.all_gather(tokens, "tensor", axis=0, tiled=True)
    outgoing = fill_slots(pair_rows, places, experts, capacity, top_k)
    received = lax.all_to_all(outgoing, "expert", split_axis=0, concat_axis=0, tiled=True)
    item_count = received.shape[1]
    partial_value = expert_partial(
        received.reshape(-1, model_width), gate_weight, up_weight, down_weight, prune_mask
    )
    whole_sum = lax.psum(partial_value.astype(jnp.bfloat16), "tensor")
    answers = whole_sum.reshape(experts, item_count, model_width)
    returned = lax.all_to_all(answers, "expert", split_axis=0, concat_axis=0, tiled=True).reshape(
        -1, model_width
    )
    member = lax.axis_index("tensor")
    own_places = lax.dynamic_slice_in_dim(places, member * tok_dev * top_k, tok_dev * top_k, 0)
    own_weights = lax.dynamic_slice_in_dim(combine, member * tok_dev, tok_dev, 0)
    picked = returned[own_places].reshape(tok_dev, top_k, model_width).astype(jnp.float32)
    mixed_out = jnp.einsum("tk,tkd->td", own_weights, picked)
    return mixed_out.astype(jnp.bfloat16)


WHOLE = pl.BlockSpec(memory_space=pltpu.VMEM)
ANYWHERE = pl.BlockSpec(memory_space=pl.ANY)


def swap(block, distance, experts):
    return lax.ppermute(block, "expert", [(i, i ^ distance) for i in range(experts)])


def swap_apart(block, even, odd, experts):
    return lax.ppermute(block, "expert", [(i, i ^ (odd if i % 2 else even)) for i in range(experts)])


def joined(a, b, loaded):
    return lax.optimization_barrier((jnp.concatenate([a, b], axis=0), loaded))


def add(*blocks):
    return functools.reduce(jnp.add, [block.astype(jnp.float32) for block in blocks]).astype(jnp.bfloat16)


def pack_kernel(tokens_ref, share_ref, out_ref):
    width = tokens_ref.shape[1]
    share = share_ref[...]
    experts = share.shape[1] // 3
    high = share.astype(jnp.bfloat16).astype(jnp.float32)
    middle = (share - high).astype(jnp.bfloat16).astype(jnp.float32)
    low = share - high - middle
    part = lax.broadcasted_iota(jnp.int32, share.shape, 1) // experts
    extra = jnp.where(part == 0, high, jnp.where(part == 1, middle, low))
    out_ref[:, :width] = tokens_ref[...]
    out_ref[:, width:] = jnp.zeros((tokens_ref.shape[0], out_ref.shape[1] - width), jnp.bfloat16)
    out_ref[:, width : width + 3 * experts] = extra.astype(jnp.bfloat16)


def load_kernel(source, after, target, sems):
    del after
    count = sems.shape[0]
    rows = source.shape[1] // count
    copies = [
        pltpu.make_async_copy(source.at[:, i * rows : (i + 1) * rows], target.at[:, i * rows : (i + 1) * rows], sems.at[i])
        for i in range(count)
    ]
    for copy in copies:
        copy.start()
    for copy in copies:
        copy.wait()


def load(source, after):
    return pl.pallas_call(
        load_kernel,
        out_shape=jax.ShapeDtypeStruct(source.shape, source.dtype),
        in_specs=[ANYWHERE] * 2,
        out_specs=WHOLE,
        scratch_shapes=[pltpu.SemaphoreType.DMA((4,))],
        cost_estimate=pl.CostEstimate(flops=0, bytes_accessed=2 * source.size, transcendentals=0),
        compiler_params=pltpu.CompilerParams(vmem_limit_bytes=1 << 20),
    )(source, after)


def expert_kernel(experts, n_pieces, *refs):
    pieces = refs[:n_pieces]
    mask_ref, gate_ref, up_ref, down_ref = refs[n_pieces : n_pieces + 4]
    answers = refs[n_pieces + 4 : 2 * n_pieces + 4]
    rows, hidden = refs[2 * n_pieces + 4 :]
    width, units = gate_ref.shape[1:]
    me = lax.axis_index("expert")
    spots, spans = [], []
    at = 0
    for piece in pieces:
        count = piece.shape[0]
        spans.append(slice(at, at + count))
        rows[at : at + count, :] = piece[:, :width]
        extra = piece[:, width:]
        lane = lax.broadcasted_iota(jnp.int32, extra.shape, 1)
        mine = (lane % experts == me) & (lane < 3 * experts)
        spots.append(jnp.sum(jnp.where(mine, extra.astype(jnp.float32), 0.0), axis=1, keepdims=True))
        at += count
    share = jnp.concatenate(spots, axis=0)
    wide = 2 * BLK if units % (2 * BLK) == 0 else BLK
    for j in range(units // wide):
        cols = slice(j * wide, (j + 1) * wide)
        gate_act = jnp.dot(rows[...], gate_ref[0, :, cols], preferred_element_type=jnp.float32)
        up_act = jnp.dot(rows[...], up_ref[0, :, cols], preferred_element_type=jnp.float32)
        block = lax.broadcasted_iota(jnp.int32, (1, wide), 1) // BLK
        keep = jnp.zeros((1, wide), jnp.float32)
        for i in range(wide // BLK):
            keep = jnp.where(block == i, mask_ref[0, j * (wide // BLK) + i].astype(jnp.float32), keep)
        value = gate_act / (1.0 + jnp.exp(-gate_act)) * up_act * keep
        hidden[:, cols] = value.astype(jnp.bfloat16)
    step = 512 if width % 512 == 0 else BLK
    for j in range(width // step):
        cols = slice(j * step, (j + 1) * step)
        answer = jnp.dot(hidden[...], down_ref[0, :, cols], preferred_element_type=jnp.float32)
        answer = (answer * share).astype(jnp.bfloat16)
        for answer_ref, span in zip(answers, spans):
            answer_ref[:, cols] = answer[span]


def dense_body(tokens, routes, combine, prune_mask, gate_weight, up_weight, down_weight):
    tok_dev, model_width = tokens.shape
    units = gate_weight.shape[2]
    experts = lax.axis_size("expert")
    lanes = jnp.arange(3 * experts, dtype=jnp.int32) % experts
    chosen = routes[:, :, None] == lanes[None, None, :]
    shares = jnp.sum(jnp.where(chosen, combine[:, :, None], 0.0), axis=1)
    packed = pl.pallas_call(
        pack_kernel,
        out_shape=jax.ShapeDtypeStruct((tok_dev, model_width + BLK), jnp.bfloat16),
        in_specs=[WHOLE] * 2,
        out_specs=WHOLE,
        compiler_params=pltpu.CompilerParams(vmem_limit_bytes=1 << 20),
    )(tokens, shares)
    own, gate_here = joined(packed, swap(packed, 8, experts), load(gate_weight, packed))
    arrived = [swap(own, distance, experts) for distance in (2, 6, 4)]
    here = [own, *arrived]
    *here, up_here, down_here = lax.optimization_barrier((*here, load(up_weight, own), load(down_weight, own)))
    pieces = here + [swap(block, 1, experts) for block in here]
    total = sum(piece.shape[0] for piece in pieces)
    answers = pl.pallas_call(
        functools.partial(expert_kernel, experts, len(pieces)),
        out_shape=[jax.ShapeDtypeStruct((piece.shape[0], model_width), jnp.bfloat16) for piece in pieces],
        in_specs=[WHOLE] * len(pieces) + [pl.BlockSpec(memory_space=pltpu.SMEM)] + [WHOLE] * 3,
        out_specs=[WHOLE] * len(pieces),
        scratch_shapes=[pltpu.VMEM((total, model_width), jnp.bfloat16), pltpu.VMEM((total, units), jnp.bfloat16)],
        compiler_params=pltpu.CompilerParams(vmem_limit_bytes=16 << 20),
    )(*pieces, prune_mask, gate_here, up_here, down_here)
    count = len(here)
    sums = [add(mine, swap(other, 1, experts)) for mine, other in zip(answers[:count], answers[count:])]
    sums = sums[:1] + [lax.optimization_barrier(block) for block in sums[1:]]
    terms = sums[:1] + [swap(block, distance, experts) for block, distance in zip(sums[1:], (2, 6, 4))]
    sent = lax.optimization_barrier(add(*[term[tok_dev:] for term in terms]))
    return add(*[term[:tok_dev] for term in terms], swap(sent, 8, experts))


def body(tokens, routes, combine, prune_mask, gate_weight, up_weight, down_weight):
    experts = lax.axis_size("expert")
    group_rows, top_k = routes.shape
    full = 2 * group_rows * top_k // experts >= group_rows
    if full and experts == 16 and lax.axis_size("tensor") == 1:
        chosen_body = dense_body
    else:
        chosen_body = slotted_body
    return chosen_body(tokens, routes, combine, prune_mask, gate_weight, up_weight, down_weight)


def solution(mesh):
    in_specs = (
        P(("groups", "expert", "tensor"), None),
        P(("groups", "expert"), None),
        P(("groups", "expert"), None),
        P("expert", "tensor"),
        P("expert", None, "tensor"),
        P("expert", None, "tensor"),
        P("expert", "tensor", None),
    )
    out_specs = P(("groups", "expert", "tensor"), None)
    return jax.shard_map(body, mesh=mesh, in_specs=in_specs, out_specs=out_specs, check_vma=False)
```

```python
import functools

import jax
import jax.numpy as jnp
from jax import lax
from jax.experimental import pallas as pl
from jax.experimental.pallas import tpu as pltpu
from jax.sharding import PartitionSpec as P

BLK = 128


def slot_places(group_routes, experts, capacity):
    flat_routes = group_routes.reshape(-1)
    onehot = (flat_routes[:, None] == jnp.arange(experts, dtype=jnp.int32)[None, :]).astype(
        jnp.int32
    )
    before = jnp.cumsum(onehot, axis=0) - onehot
    slot_index = jnp.sum(before * onehot, axis=1)
    return flat_routes * capacity + slot_index


def fill_slots(row_source, places, experts, capacity, top_k):
    owners = jnp.full((experts * capacity,), -1, jnp.int32)
    owners = owners.at[places].set(jnp.arange(places.shape[0], dtype=jnp.int32) // top_k)
    filled = owners >= 0
    outgoing = row_source[jnp.maximum(owners, 0)]
    outgoing = jnp.where(filled[:, None], outgoing, jnp.zeros_like(outgoing))
    return outgoing.reshape(experts, capacity, row_source.shape[1])


def expert_partial(row_block, gate_weight, up_weight, down_weight, prune_mask):
    keep_cols = jnp.repeat(prune_mask[0].astype(jnp.float32), BLK)
    gate_act = jnp.dot(row_block, gate_weight[0], preferred_element_type=jnp.float32)
    up_act = jnp.dot(row_block, up_weight[0], preferred_element_type=jnp.float32)
    hidden = (jax.nn.silu(gate_act) * up_act * keep_cols).astype(jnp.bfloat16)
    partial_value = jnp.dot(hidden, down_weight[0], preferred_element_type=jnp.float32)
    rounded = lax.optimization_barrier(partial_value.astype(jnp.bfloat16))
    return rounded.astype(jnp.float32)


def slotted_body(tokens, routes, combine, prune_mask, gate_weight, up_weight, down_weight):
    tok_dev, model_width = tokens.shape
    group_rows, top_k = routes.shape
    experts = lax.axis_size("expert")
    capacity = min(group_rows, 2 * group_rows * top_k // experts)
    places = slot_places(routes, experts, capacity)
    pair_rows = lax.all_gather(tokens, "tensor", axis=0, tiled=True)
    outgoing = fill_slots(pair_rows, places, experts, capacity, top_k)
    received = lax.all_to_all(outgoing, "expert", split_axis=0, concat_axis=0, tiled=True)
    item_count = received.shape[1]
    partial_value = expert_partial(
        received.reshape(-1, model_width), gate_weight, up_weight, down_weight, prune_mask
    )
    whole_sum = lax.psum(partial_value.astype(jnp.bfloat16), "tensor")
    answers = whole_sum.reshape(experts, item_count, model_width)
    returned = lax.all_to_all(answers, "expert", split_axis=0, concat_axis=0, tiled=True).reshape(
        -1, model_width
    )
    member = lax.axis_index("tensor")
    own_places = lax.dynamic_slice_in_dim(places, member * tok_dev * top_k, tok_dev * top_k, 0)
    own_weights = lax.dynamic_slice_in_dim(combine, member * tok_dev, tok_dev, 0)
    picked = returned[own_places].reshape(tok_dev, top_k, model_width).astype(jnp.float32)
    mixed_out = jnp.einsum("tk,tkd->td", own_weights, picked)
    return mixed_out.astype(jnp.bfloat16)


WHOLE = pl.BlockSpec(memory_space=pltpu.VMEM)
ANYWHERE = pl.BlockSpec(memory_space=pl.ANY)


def swap(block, distance, experts):
    return lax.ppermute(block, "expert", [(i, i ^ distance) for i in range(experts)])


def swap_apart(block, even, odd, experts):
    return lax.ppermute(block, "expert", [(i, i ^ (odd if i % 2 else even)) for i in range(experts)])


def joined(a, b, loaded):
    return lax.optimization_barrier((jnp.concatenate([a, b], axis=0), loaded))


def add(*blocks):
    return functools.reduce(jnp.add, [block.astype(jnp.float32) for block in blocks]).astype(jnp.bfloat16)


def pack_kernel(tokens_ref, share_ref, out_ref):
    width = tokens_ref.shape[1]
    share = share_ref[...]
    experts = share.shape[1] // 3
    high = share.astype(jnp.bfloat16).astype(jnp.float32)
    middle = (share - high).astype(jnp.bfloat16).astype(jnp.float32)
    low = share - high - middle
    part = lax.broadcasted_iota(jnp.int32, share.shape, 1) // experts
    extra = jnp.where(part == 0, high, jnp.where(part == 1, middle, low))
    out_ref[:, :width] = tokens_ref[...]
    out_ref[:, width:] = jnp.zeros((tokens_ref.shape[0], out_ref.shape[1] - width), jnp.bfloat16)
    out_ref[:, width : width + 3 * experts] = extra.astype(jnp.bfloat16)


def load_kernel(source, after, target, sems):
    del after
    count = sems.shape[0]
    rows = source.shape[1] // count
    copies = [
        pltpu.make_async_copy(source.at[:, i * rows : (i + 1) * rows], target.at[:, i * rows : (i + 1) * rows], sems.at[i])
        for i in range(count)
    ]
    for copy in copies:
        copy.start()
    for copy in copies:
        copy.wait()


def load(source, after):
    return pl.pallas_call(
        load_kernel,
        out_shape=jax.ShapeDtypeStruct(source.shape, source.dtype),
        in_specs=[ANYWHERE] * 2,
        out_specs=WHOLE,
        scratch_shapes=[pltpu.SemaphoreType.DMA((4,))],
        cost_estimate=pl.CostEstimate(flops=0, bytes_accessed=2 * source.size, transcendentals=0),
        compiler_params=pltpu.CompilerParams(vmem_limit_bytes=1 << 20),
    )(source, after)


def expert_kernel(experts, n_pieces, *refs):
    pieces = refs[:n_pieces]
    mask_ref, gate_ref, up_ref, down_ref = refs[n_pieces : n_pieces + 4]
    *answers, rows, hidden = refs[n_pieces + 4 :]
    width, units = gate_ref.shape[1:]
    me = lax.axis_index("expert")
    spots = []
    at = 0
    for piece in pieces:
        count = piece.shape[0]
        rows[at : at + count, :] = piece[:, :width]
        extra = piece[:, width:]
        lane = lax.broadcasted_iota(jnp.int32, extra.shape, 1)
        mine = (lane % experts == me) & (lane < 3 * experts)
        spots.append(jnp.sum(jnp.where(mine, extra.astype(jnp.float32), 0.0), axis=1, keepdims=True))
        at += count
    share = jnp.concatenate(spots, axis=0)
    wide = 2 * BLK if units % (2 * BLK) == 0 else BLK
    for j in range(units // wide):
        cols = slice(j * wide, (j + 1) * wide)
        gate_act = jnp.dot(rows[...], gate_ref[0, :, cols], preferred_element_type=jnp.float32)
        up_act = jnp.dot(rows[...], up_ref[0, :, cols], preferred_element_type=jnp.float32)
        block = lax.broadcasted_iota(jnp.int32, (1, wide), 1) // BLK
        keep = jnp.zeros((1, wide), jnp.float32)
        for i in range(wide // BLK):
            keep = jnp.where(block == i, mask_ref[0, j * (wide // BLK) + i].astype(jnp.float32), keep)
        value = gate_act / (1.0 + jnp.exp(-gate_act)) * up_act * keep
        hidden[:, cols] = value.astype(jnp.bfloat16)
    step = 512 if width % 512 == 0 else BLK
    for j in range(width // step):
        cols = slice(j * step, (j + 1) * step)
        answer = jnp.dot(hidden[...], down_ref[0, :, cols], preferred_element_type=jnp.float32)
        answer = (answer * share).astype(jnp.bfloat16)
        at = 0
        for answer_ref in answers:
            answer_ref[:, cols] = answer[at : at + answer_ref.shape[0]]
            at += answer_ref.shape[0]


def dense_body(tokens, routes, combine, prune_mask, gate_weight, up_weight, down_weight):
    tok_dev, model_width = tokens.shape
    units = gate_weight.shape[2]
    experts = lax.axis_size("expert")
    lanes = jnp.arange(3 * experts, dtype=jnp.int32) % experts
    chosen = routes[:, :, None] == lanes[None, None, :]
    shares = jnp.sum(jnp.where(chosen, combine[:, :, None], 0.0), axis=1)
    packed = pl.pallas_call(
        pack_kernel,
        out_shape=jax.ShapeDtypeStruct((tok_dev, model_width + BLK), jnp.bfloat16),
        in_specs=[WHOLE] * 2,
        out_specs=WHOLE,
        compiler_params=pltpu.CompilerParams(vmem_limit_bytes=1 << 20),
    )(tokens, shares)
    own, gate_here = joined(packed, swap(packed, 8, experts), load(gate_weight, packed))
    order = (4, 2, 6)
    arrived = {distance: swap(own, distance, experts) for distance in order}
    own_far = swap(own, 1, experts)
    last, first = order[0], order[2]
    first_far = swap(arrived[first], 1, experts)
    arrived[last], own_far, first_far, up_here, down_here = lax.optimization_barrier(
        (arrived[last], own_far, first_far, load(up_weight, own), load(down_weight, own))
    )
    far = {distance: swap(arrived[distance], 1, experts) for distance in order[:2]}
    far[first] = first_far
    pieces = [own, *[arrived[d] for d in (2, 6, 4)], far[(2, 6, 4)[0]], own_far, *[far[d] for d in (2, 6, 4)[1:]]]
    total = sum(piece.shape[0] for piece in pieces)
    block = own.shape[0]
    heights = [block] * 5 + [3 * block]
    *mine, first_far, rest_far = pl.pallas_call(
        functools.partial(expert_kernel, experts, len(pieces)),
        out_shape=[jax.ShapeDtypeStruct((height, model_width), jnp.bfloat16) for height in heights],
        in_specs=[WHOLE] * len(pieces) + [pl.BlockSpec(memory_space=pltpu.SMEM)] + [WHOLE] * 3,
        out_specs=[WHOLE] * len(heights),
        scratch_shapes=[pltpu.VMEM((total, model_width), jnp.bfloat16), pltpu.VMEM((total, units), jnp.bfloat16)],
        compiler_params=pltpu.CompilerParams(vmem_limit_bytes=16 << 20),
    )(*pieces, prune_mask, gate_here, up_here, down_here)
    first_far, rest_far = swap(first_far, 1, experts), swap(rest_far, 1, experts)
    others = [rest_far[:block], first_far, rest_far[block : 2 * block], rest_far[2 * block :]]
    sums = [add(here, there) for here, there in zip(mine, others)]
    sums = sums[:1] + [lax.optimization_barrier(one) for one in sums[1:]]
    terms = sums[:1] + [swap(one, distance, experts) for one, distance in zip(sums[1:], (2, 6, 4))]
    sent = lax.optimization_barrier(add(*[term[tok_dev:] for term in terms]))
    return add(*[term[:tok_dev] for term in terms], swap(sent, 8, experts))


def body(tokens, routes, combine, prune_mask, gate_weight, up_weight, down_weight):
    experts = lax.axis_size("expert")
    group_rows, top_k = routes.shape
    full = 2 * group_rows * top_k // experts >= group_rows
    if full and experts == 16 and lax.axis_size("tensor") == 1:
        chosen_body = dense_body
    else:
        chosen_body = slotted_body
    return chosen_body(tokens, routes, combine, prune_mask, gate_weight, up_weight, down_weight)


def solution(mesh):
    in_specs = (
        P(("groups", "expert", "tensor"), None),
        P(("groups", "expert"), None),
        P(("groups", "expert"), None),
        P("expert", "tensor"),
        P("expert", None, "tensor"),
        P("expert", None, "tensor"),
        P("expert", "tensor", None),
    )
    out_specs = P(("groups", "expert", "tensor"), None)
    return jax.shard_map(body, mesh=mesh, in_specs=in_specs, out_specs=out_specs, check_vma=False)
```

```python
import functools

import jax
import jax.numpy as jnp
from jax import lax
from jax.experimental import pallas as pl
from jax.experimental.pallas import tpu as pltpu
from jax.sharding import PartitionSpec as P

BLK = 128


def slot_places(group_routes, experts, capacity):
    flat_routes = group_routes.reshape(-1)
    onehot = (flat_routes[:, None] == jnp.arange(experts, dtype=jnp.int32)[None, :]).astype(
        jnp.int32
    )
    before = jnp.cumsum(onehot, axis=0) - onehot
    slot_index = jnp.sum(before * onehot, axis=1)
    return flat_routes * capacity + slot_index


def fill_slots(row_source, places, experts, capacity, top_k):
    owners = jnp.full((experts * capacity,), -1, jnp.int32)
    owners = owners.at[places].set(jnp.arange(places.shape[0], dtype=jnp.int32) // top_k)
    filled = owners >= 0
    outgoing = row_source[jnp.maximum(owners, 0)]
    outgoing = jnp.where(filled[:, None], outgoing, jnp.zeros_like(outgoing))
    return outgoing.reshape(experts, capacity, row_source.shape[1])


def expert_partial(row_block, gate_weight, up_weight, down_weight, prune_mask):
    keep_cols = jnp.repeat(prune_mask[0].astype(jnp.float32), BLK)
    gate_act = jnp.dot(row_block, gate_weight[0], preferred_element_type=jnp.float32)
    up_act = jnp.dot(row_block, up_weight[0], preferred_element_type=jnp.float32)
    hidden = (jax.nn.silu(gate_act) * up_act * keep_cols).astype(jnp.bfloat16)
    partial_value = jnp.dot(hidden, down_weight[0], preferred_element_type=jnp.float32)
    rounded = lax.optimization_barrier(partial_value.astype(jnp.bfloat16))
    return rounded.astype(jnp.float32)


def slotted_body(tokens, routes, combine, prune_mask, gate_weight, up_weight, down_weight):
    tok_dev, model_width = tokens.shape
    group_rows, top_k = routes.shape
    experts = lax.axis_size("expert")
    capacity = min(group_rows, 2 * group_rows * top_k // experts)
    places = slot_places(routes, experts, capacity)
    pair_rows = lax.all_gather(tokens, "tensor", axis=0, tiled=True)
    outgoing = fill_slots(pair_rows, places, experts, capacity, top_k)
    received = lax.all_to_all(outgoing, "expert", split_axis=0, concat_axis=0, tiled=True)
    item_count = received.shape[1]
    partial_value = expert_partial(
        received.reshape(-1, model_width), gate_weight, up_weight, down_weight, prune_mask
    )
    whole_sum = lax.psum(partial_value.astype(jnp.bfloat16), "tensor")
    answers = whole_sum.reshape(experts, item_count, model_width)
    returned = lax.all_to_all(answers, "expert", split_axis=0, concat_axis=0, tiled=True).reshape(
        -1, model_width
    )
    member = lax.axis_index("tensor")
    own_places = lax.dynamic_slice_in_dim(places, member * tok_dev * top_k, tok_dev * top_k, 0)
    own_weights = lax.dynamic_slice_in_dim(combine, member * tok_dev, tok_dev, 0)
    picked = returned[own_places].reshape(tok_dev, top_k, model_width).astype(jnp.float32)
    mixed_out = jnp.einsum("tk,tkd->td", own_weights, picked)
    return mixed_out.astype(jnp.bfloat16)


WHOLE = pl.BlockSpec(memory_space=pltpu.VMEM)
ANYWHERE = pl.BlockSpec(memory_space=pl.ANY)


def swap(block, distance, experts):
    return lax.ppermute(block, "expert", [(i, i ^ distance) for i in range(experts)])


def swap_apart(block, even, odd, experts):
    return lax.ppermute(block, "expert", [(i, i ^ (odd if i % 2 else even)) for i in range(experts)])


def joined(a, b, loaded):
    return lax.optimization_barrier((jnp.concatenate([a, b], axis=0), loaded))


def add(*blocks):
    return functools.reduce(jnp.add, [block.astype(jnp.float32) for block in blocks]).astype(jnp.bfloat16)


def pack_kernel(tokens_ref, share_ref, out_ref):
    width = tokens_ref.shape[1]
    share = share_ref[...]
    experts = share.shape[1] // 3
    high = share.astype(jnp.bfloat16).astype(jnp.float32)
    middle = (share - high).astype(jnp.bfloat16).astype(jnp.float32)
    low = share - high - middle
    part = lax.broadcasted_iota(jnp.int32, share.shape, 1) // experts
    extra = jnp.where(part == 0, high, jnp.where(part == 1, middle, low))
    out_ref[:, :width] = tokens_ref[...]
    out_ref[:, width:] = jnp.zeros((tokens_ref.shape[0], out_ref.shape[1] - width), jnp.bfloat16)
    out_ref[:, width : width + 3 * experts] = extra.astype(jnp.bfloat16)


def load_kernel(source, after, target, sems):
    del after
    count = sems.shape[0]
    rows = source.shape[1] // count
    copies = [
        pltpu.make_async_copy(source.at[:, i * rows : (i + 1) * rows], target.at[:, i * rows : (i + 1) * rows], sems.at[i])
        for i in range(count)
    ]
    for copy in copies:
        copy.start()
    for copy in copies:
        copy.wait()


def load(source, after):
    return pl.pallas_call(
        load_kernel,
        out_shape=jax.ShapeDtypeStruct(source.shape, source.dtype),
        in_specs=[ANYWHERE] * 2,
        out_specs=WHOLE,
        scratch_shapes=[pltpu.SemaphoreType.DMA((4,))],
        cost_estimate=pl.CostEstimate(flops=0, bytes_accessed=2 * source.size, transcendentals=0),
        compiler_params=pltpu.CompilerParams(vmem_limit_bytes=1 << 20),
    )(source, after)


def expert_kernel(experts, n_pieces, *refs):
    own, four, six, two, own_far, four_far, six_far, two_far = (piece[...] for piece in refs[:n_pieces])
    second = lax.axis_index("expert") % 2 == 1
    duty = [jnp.where(second, six, four), jnp.where(second, six_far, four_far)]
    given = [jnp.where(second, four_far, six_far), jnp.where(second, four, six)]
    pieces = [own, two, *duty, own_far, *given, two_far]
    mask_ref, gate_ref, up_ref, down_ref = refs[n_pieces : n_pieces + 4]
    *answers, rows, hidden = refs[n_pieces + 4 :]
    width, units = gate_ref.shape[1:]
    me = lax.axis_index("expert")
    spots = []
    at = 0
    for piece in pieces:
        count = piece.shape[0]
        rows[at : at + count, :] = piece[:, :width]
        extra = piece[:, width:]
        lane = lax.broadcasted_iota(jnp.int32, extra.shape, 1)
        mine = (lane % experts == me) & (lane < 3 * experts)
        spots.append(jnp.sum(jnp.where(mine, extra.astype(jnp.float32), 0.0), axis=1, keepdims=True))
        at += count
    share = jnp.concatenate(spots, axis=0)
    wide = 2 * BLK if units % (2 * BLK) == 0 else BLK
    for j in range(units // wide):
        cols = slice(j * wide, (j + 1) * wide)
        gate_act = jnp.dot(rows[...], gate_ref[0, :, cols], preferred_element_type=jnp.float32)
        up_act = jnp.dot(rows[...], up_ref[0, :, cols], preferred_element_type=jnp.float32)
        block = lax.broadcasted_iota(jnp.int32, (1, wide), 1) // BLK
        keep = jnp.zeros((1, wide), jnp.float32)
        for i in range(wide // BLK):
            keep = jnp.where(block == i, mask_ref[0, j * (wide // BLK) + i].astype(jnp.float32), keep)
        value = gate_act / (1.0 + jnp.exp(-gate_act)) * up_act * keep
        hidden[:, cols] = value.astype(jnp.bfloat16)
    step = 512 if width % 512 == 0 else BLK
    for j in range(width // step):
        cols = slice(j * step, (j + 1) * step)
        answer = jnp.dot(hidden[...], down_ref[0, :, cols], preferred_element_type=jnp.float32)
        answer = (answer * share).astype(jnp.bfloat16)
        at = 0
        for answer_ref in answers:
            answer_ref[:, cols] = answer[at : at + answer_ref.shape[0]]
            at += answer_ref.shape[0]


def dense_body(tokens, routes, combine, prune_mask, gate_weight, up_weight, down_weight):
    tok_dev, model_width = tokens.shape
    units = gate_weight.shape[2]
    experts = lax.axis_size("expert")
    lanes = jnp.arange(3 * experts, dtype=jnp.int32) % experts
    chosen = routes[:, :, None] == lanes[None, None, :]
    shares = jnp.sum(jnp.where(chosen, combine[:, :, None], 0.0), axis=1)
    packed = pl.pallas_call(
        pack_kernel,
        out_shape=jax.ShapeDtypeStruct((tok_dev, model_width + BLK), jnp.bfloat16),
        in_specs=[WHOLE] * 2,
        out_specs=WHOLE,
        compiler_params=pltpu.CompilerParams(vmem_limit_bytes=1 << 20),
    )(tokens, shares)
    own, gate_here = joined(packed, swap(packed, 8, experts), load(gate_weight, packed))
    order = (4, 6, 2)
    arrived = {distance: swap(own, distance, experts) for distance in order}
    own_far = swap(own, 1, experts)
    last, first = order[0], order[2]
    first_far = swap(arrived[first], 1, experts)
    arrived[last], own_far, first_far, up_here, down_here = lax.optimization_barrier(
        (arrived[last], own_far, first_far, load(up_weight, own), load(down_weight, own))
    )
    far = {distance: swap(arrived[distance], 1, experts) for distance in order[:2]}
    far[first] = first_far
    pieces = [own, arrived[2], arrived[4], arrived[6], own_far, far[2], far[4], far[6]]
    total = sum(piece.shape[0] for piece in pieces)
    block = own.shape[0]
    heights = [block, block, 2 * block, block, 2 * block, block]
    own, two, duty, own_far, given, two_far = pl.pallas_call(
        functools.partial(expert_kernel, experts, len(pieces)),
        out_shape=[jax.ShapeDtypeStruct((height, model_width), jnp.bfloat16) for height in heights],
        in_specs=[WHOLE] * len(pieces) + [pl.BlockSpec(memory_space=pltpu.SMEM)] + [WHOLE] * 3,
        out_specs=[WHOLE] * len(heights),
        scratch_shapes=[pltpu.VMEM((total, model_width), jnp.bfloat16), pltpu.VMEM((total, units), jnp.bfloat16)],
        compiler_params=pltpu.CompilerParams(vmem_limit_bytes=16 << 20),
    )(*pieces, prune_mask, gate_here, up_here, down_here)
    duty = lax.optimization_barrier(add(duty, swap(given, 1, experts)))
    two = lax.optimization_barrier(add(two, swap(two_far, 1, experts)))
    duty, two = swap_apart(duty, 2, 4, experts), swap(two, 6, experts)
    own_far = swap(lax.optimization_barrier(add(own_far, duty[block:])), 1, experts)
    terms = [own, duty[:block], two, own_far]
    sent = lax.optimization_barrier(add(*[term[tok_dev:] for term in terms]))
    return add(*[term[:tok_dev] for term in terms], swap(sent, 8, experts))


def body(tokens, routes, combine, prune_mask, gate_weight, up_weight, down_weight):
    experts = lax.axis_size("expert")
    group_rows, top_k = routes.shape
    full = 2 * group_rows * top_k // experts >= group_rows
    if full and experts == 16 and lax.axis_size("tensor") == 1:
        chosen_body = dense_body
    else:
        chosen_body = slotted_body
    return chosen_body(tokens, routes, combine, prune_mask, gate_weight, up_weight, down_weight)


def solution(mesh):
    in_specs = (
        P(("groups", "expert", "tensor"), None),
        P(("groups", "expert"), None),
        P(("groups", "expert"), None),
        P("expert", "tensor"),
        P("expert", None, "tensor"),
        P("expert", None, "tensor"),
        P("expert", "tensor", None),
    )
    out_specs = P(("groups", "expert", "tensor"), None)
    return jax.shard_map(body, mesh=mesh, in_specs=in_specs, out_specs=out_specs, check_vma=False)
```
